32 devices in a mesh: dp: 8 (over z, y), block: 4 (over x, core).
Axes of the slice: x: 2, y: 2, z: 4, core: 2. Of those that a mesh axis runs over, the one named last changes fastest.
Arguments:
- x_act: bfloat16 [4, 4096, 4096], P('block', 'dp')
- g_out: bfloat16 [4, 4096, 4096], P('block', 'dp')
- proj_in: bfloat16 [4, 4096, 64], P('block'), may hold values from -0.09375 to 0.09375
- proj_out: bfloat16 [4, 4096, 64], P('block'), may hold values from -0.09375 to 0.09375
- queries: bfloat16 [4, 512, 4096], P('block', 'dp'), may hold values from -6 to 6
- cand_ids: int32 [8, 8, 2], P('dp'), may hold values from 0 to 15, as said below
- cand_counts: int32 [8, 8], P('dp'), may hold values from 0 to 2, as said below
Outputs:
- scores: float32 [512, 32], P(('dp', 'block'))
The draws below stay inside these ranges and needn't reach their ends.
Inputs may be any that keep to these rules, and one draw needn't show every extreme that they name: `cand_ids`: each list of a training shard d for an owner p names 2 distinct query blocks of p; slots at or past cand_counts[d, p] are padding. Every training shard d has cand_counts[d, d] = 2.
All inputs are finite; a program needn't handle non-finite values.
Results may differ from the reference program's by a relative error of at most 0.0096.
Values may be sent and summed in bfloat16 or wider, within the bound.
A program may use at most 64 MiB of HBM per device.

```python
import math
import jax
import jax.numpy as jnp
from jax import lax

D = 4096
R = 64
E_DEV = 4
SEQ = 128
Q_DEV = 64
QB = 4
CAP = 2
LAYERS = 4
TRAIN = 32
TOKENS = 4096
QUERIES = 512
QBO = 16


def draw_stream(key, salt):
    stream_key = jax.random.fold_in(key, salt)
    subkeys = jax.random.split(stream_key, 12)
    shape = (LAYERS, TOKENS, D)
    rising = 1.0 + 2.0 * jnp.arange(TOKENS, dtype=jnp.float32) / max(TOKENS - 1, 1)
    rising = rising[None, :, None]
    noise = jax.random.normal(subkeys[0], shape, jnp.float32)
    row_scale = jnp.ones((LAYERS, TOKENS, 1), jnp.float32)
    shared = jnp.zeros(shape, jnp.float32)
    for component in range(4):
        token_coef = jax.random.normal(subkeys[2 + 2 * component], (LAYERS, TOKENS, 1), jnp.float32)
        feature_dir = jax.random.normal(subkeys[3 + 2 * component], (LAYERS, 1, D), jnp.float32)
        shared = shared + token_coef * feature_dir
    return (rising * row_scale * (noise + shared)).astype(jnp.bfloat16)


def draw_x_act(key, part):
    return draw_stream(key, 101)


def draw_g_out(key, part):
    return draw_stream(key, 202)


def candidate_tables(key):
    owners = QUERIES // Q_DEV
    perm_keys = jax.random.split(jax.random.fold_in(key, 7), owners * owners)
    perms = jax.vmap(lambda subkey: jax.random.permutation(subkey, QBO))(perm_keys)
    id_table = perms[:, :CAP].reshape(owners, owners, CAP).astype(jnp.int32)
    base_count = jax.random.randint(jax.random.fold_in(key, 11), (owners, owners), 0, CAP + 1)
    heat = jax.random.randint(jax.random.fold_in(key, 13), (1, owners), 0, 3)
    counts = jnp.clip(base_count + heat - 1, 0, CAP)
    counts = jnp.where(jnp.eye(owners, dtype=bool), CAP, counts).astype(jnp.int32)
    return (id_table, counts)


def draw_cand_ids(key, part):
    return candidate_tables(key)[0]


def draw_cand_counts(key, part):
    return candidate_tables(key)[1]


def shard_levels(key, shape, cuts, least, largest):
    factor_of = 1.0
    for dim, parts in cuts:
        heights = jax.random.uniform(jax.random.fold_in(jax.random.fold_in(key, 6), dim), (parts,), jnp.float32, least / len(cuts), largest / len(cuts))
        factor_of = factor_of * jnp.repeat(jnp.exp(heights), shape[dim] // parts).reshape((-1,) + (1,) * (len(shape) - 1 - dim))
    return factor_of


def centred(key, dims, scale, most, cuts=(), kind=jnp.bfloat16):
    level = shard_levels(key, dims, cuts, -0.22, 0.18) if cuts else 1.0
    values = jax.random.normal(key, dims, jnp.float32) * scale * level
    return jnp.minimum(jnp.maximum(values, -most), most).astype(kind)


def setup_inputs(seed: int = 0) -> dict:
    arg_keys = jax.random.split(jax.random.key(seed), 8)
    return {
        "x_act": draw_x_act(jax.random.fold_in(arg_keys[7], 71), 0),
        "g_out": draw_g_out(jax.random.fold_in(arg_keys[7], 71), 0),
        "proj_in": centred(arg_keys[2], (LAYERS, D, R), D ** -0.5, 0.09375, ((0, 4),)),
        "proj_out": centred(arg_keys[3], (LAYERS, D, R), D ** -0.5, 0.09375, ((0, 4),)),
        "queries": centred(arg_keys[4], (LAYERS, QUERIES, R * R), 1.0, 6.0, ((0, 4), (1, 8))),
        "cand_ids": draw_cand_ids(jax.random.fold_in(arg_keys[7], 71), 0),
        "cand_counts": draw_cand_counts(jax.random.fold_in(arg_keys[7], 71), 0),
    }


DAMP = 0.1

def kron_inverse(factor):
    width = factor.shape[0]
    identity = jnp.eye(width, dtype=jnp.float32)
    damping = DAMP * jnp.trace(factor) / width + 1e-06
    lower_factor = jnp.linalg.cholesky(factor + damping * identity)
    return jax.scipy.linalg.cho_solve((lower_factor, True), identity)

def reference(x_act, g_out, proj_in, proj_out, queries, cand_ids, cand_counts):
    score_sum = jnp.zeros((QUERIES, TRAIN), jnp.float32)
    for layer_idx in range(LAYERS):
        act_proj = jnp.dot(x_act[layer_idx].astype(jnp.float32), proj_in[layer_idx].astype(jnp.float32), preferred_element_type=jnp.float32).astype(jnp.bfloat16)
        grad_proj = jnp.dot(g_out[layer_idx].astype(jnp.float32), proj_out[layer_idx].astype(jnp.float32), preferred_element_type=jnp.float32).astype(jnp.bfloat16)
        factor_a = jnp.dot(act_proj.T.astype(jnp.float32), act_proj.astype(jnp.float32), preferred_element_type=jnp.float32) / TOKENS
        factor_g = jnp.dot(grad_proj.T.astype(jnp.float32), grad_proj.astype(jnp.float32), preferred_element_type=jnp.float32) / TOKENS
        inverse_a = kron_inverse(factor_a)
        inverse_g = kron_inverse(factor_g)
        act_three = act_proj.astype(jnp.float32).reshape(TRAIN, SEQ, R)
        grad_three = grad_proj.astype(jnp.float32).reshape(TRAIN, SEQ, R)
        example_grad = jnp.einsum('esi,esj->eij', grad_three, act_three, precision=lax.Precision.HIGHEST) / SEQ
        left_side = jnp.einsum('ij,ejk->eik', inverse_g, example_grad, precision=lax.Precision.HIGHEST)
        precond = jnp.einsum('eik,kl->eil', left_side, inverse_a, precision=lax.Precision.HIGHEST)
        precond = precond.reshape(TRAIN, R * R).astype(jnp.bfloat16)
        score_sum = score_sum + lax.dot_general(queries[layer_idx].astype(jnp.float32), precond.astype(jnp.float32), (((1,), (1,)), ((), ())), preferred_element_type=jnp.float32)
    owners = QUERIES // Q_DEV
    slot_live = jnp.arange(CAP)[None, None, :] < cand_counts[:, :, None]
    matches = (cand_ids[:, :, :, None] == jnp.arange(QBO)[None, None, None, :]) & slot_live[:, :, :, None]
    live = jnp.any(matches, axis=2).astype(jnp.float32)
    mask_blocks = jnp.transpose(live, (1, 2, 0))
    mask = jnp.broadcast_to(mask_blocks[:, :, None, :, None], (owners, QBO, QB, owners, E_DEV)).reshape(QUERIES, TRAIN)
    scale = 1.0 / math.sqrt(R * R * LAYERS)
    return score_sum * scale * mask
```

```python
import functools

import jax
import jax.numpy as jnp
from jax import lax
from jax.experimental import pallas as pl
from jax.experimental.pallas import tpu as pltpu
from jax.sharding import PartitionSpec as P

E_DEV = 4
SEQ = 128
QB = 4
CAP = 2
DAMP = 0.1
MESH = pl.DeviceIdType.MESH
HIGHEST = lax.Precision.HIGHEST


def dot(lhs, rhs, dims=(1, 0), precision=None):
    return lax.dot_general(
        lhs,
        rhs,
        (((dims[0],), (dims[1],)), ((), ())),
        preferred_element_type=jnp.float32,
        precision=precision,
    )


def kron_inverses(packed, width):
    shape = packed.shape
    lane_all = lax.broadcasted_iota(jnp.int32, shape, 1)
    first = lane_all < width
    lane = jnp.where(first, lane_all, lane_all - width)
    sub = lax.broadcasted_iota(jnp.int32, shape, 0)
    diag = jnp.sum(jnp.where(lane == sub, packed, 0.0), axis=0, keepdims=True)
    first_row = first[0:1]
    trace_a = jnp.sum(jnp.where(first_row, diag, 0.0), axis=1, keepdims=True)
    trace_g = jnp.sum(jnp.where(first_row, 0.0, diag), axis=1, keepdims=True)
    damping = DAMP * jnp.where(first_row, trace_a, trace_g) / width + 1e-06
    mat = packed + jnp.where(lane == sub, damping, 0.0)
    lane_row = lane[0:1]

    def column(k):
        col_a = jnp.broadcast_to(mat[:, k : k + 1], shape)
        col_g = jnp.broadcast_to(mat[:, width + k : width + k + 1], shape)
        return jnp.where(first, col_a, col_g)

    for k in range(0, width, 2):
        col0, col1 = column(k), column(k + 1)
        p00, p01, p11 = col0[k : k + 1], col0[k + 1 : k + 2], col1[k + 1 : k + 2]
        inv_det = 1.0 / (p00 * p11 - p01 * p01)
        at0, at1 = lane_row == k, lane_row == k + 1
        row0 = jnp.where(at0, 1.0, jnp.where(at1, 0.0, mat[k : k + 1]))
        row1 = jnp.where(at1, 1.0, jnp.where(at0, 0.0, mat[k + 1 : k + 2]))
        new0 = (p11 * row0 - p01 * row1) * inv_det
        new1 = (p00 * row1 - p01 * row0) * inv_det
        in0, in1 = sub == k, sub == k + 1
        keep = jnp.where((lane == k) | (lane == k + 1) | in0 | in1, 0.0, mat)
        mul0 = jnp.where(in0, -1.0, jnp.where(in1, 0.0, col0))
        mul1 = jnp.where(in1, -1.0, jnp.where(in0, 0.0, col1))
        mat = keep - mul0 * new0 - mul1 * new1
    return mat


def kernel(
    n, layers, x_hbm, g_hbm, pin_hbm, pout_hbm, q_hbm, ids_ref, counts_ref, out_ref,
    xbuf, gbuf, pin, pout, qbuf, fsend, frecv, fred, fall, tg_ref, flat_src, flat, tbuf,
    part, sbuf, load_x, load_g, load_p, send1, recv1, send2, recv2, send_a, recv_a,
    send_b, recv_b, send_s, recv_s,
):
    me = lax.axis_index("dp")
    layer = lax.axis_index("block")
    width = pin.shape[0]
    lanes = 2 * width
    owned = qbuf.shape[0]
    rows = width // n
    chunks = 16 // E_DEV
    chunk = tbuf.shape[2]

    loads = []
    pin_copy = pltpu.make_async_copy(pin_hbm, pin, load_p.at[0])
    pout_copy = pltpu.make_async_copy(pout_hbm, pout, load_p.at[1])
    q_copy = pltpu.make_async_copy(q_hbm, qbuf, load_p.at[2])
    pin_copy.start()
    pout_copy.start()
    for e in range(E_DEV):
        span = pl.ds(e * SEQ, SEQ)
        x_copy = pltpu.make_async_copy(x_hbm.at[span], xbuf.at[e], load_x.at[e])
        g_copy = pltpu.make_async_copy(g_hbm.at[span], gbuf.at[e], load_g.at[e])
        x_copy.start()
        g_copy.start()
        loads.append((x_copy, g_copy))
    q_copy.start()

    barrier = pltpu.get_barrier_semaphore()
    for o in range(1, n):
        pl.semaphore_signal(
            barrier, inc=1, device_id=(lax.rem(me + o, n), layer), device_id_type=MESH
        )
    for o in range(1, layers):
        pl.semaphore_signal(
            barrier, inc=1, device_id=(me, lax.rem(layer + o, layers)), device_id_type=MESH
        )

    lane_q = lax.broadcasted_iota(jnp.int32, (8, lanes), 1) // QB
    for p in range(n):
        live = jnp.zeros((8, lanes), jnp.float32)
        for s in range(CAP):
            wanted = jnp.where(s < counts_ref[0, p], ids_ref[s, p], -1)
            live = jnp.where(lane_q == wanted, 1.0, live)
        fsend[p, 8 * pl.cdiv(rows, 8) :, :] = live

    pin_copy.wait()
    pout_copy.wait()
    grams = jnp.zeros((lanes, lanes), jnp.float32)
    for e in range(E_DEV):
        loads[e][0].wait()
        act = dot(xbuf[e], pin[...], (1, 1))
        loads[e][1].wait()
        grad = dot(gbuf[e], pout[...], (1, 1))
        both = jnp.concatenate([act, grad], axis=1).astype(jnp.bfloat16)
        gram = dot(both, both, (0, 0))
        tg_ref[e * width : (e + 1) * width, :] = gram[width:, :width] * (1.0 / SEQ)
        grams = grams + gram
    lane_sq = lax.broadcasted_iota(jnp.int32, (width, lanes), 1)
    first = lane_sq < width
    factors = jnp.where(first, grams[:width], grams[width:])
    for p in range(n):
        fsend[p, 0:rows, :] = factors[p * rows : (p + 1) * rows]

    pl.semaphore_wait(barrier, n - 1 + layers - 1)

    def to_dp(src, dst, send, recv, peer):
        return pltpu.make_async_remote_copy(
            src_ref=src, dst_ref=dst, send_sem=send, recv_sem=recv,
            device_id=(peer, layer), device_id_type=MESH,
        )

    first_copies = []
    for o in range(1, n):
        peer = lax.rem(me + o, n)
        copy = to_dp(fsend.at[peer], frecv.at[me], send1.at[o], recv1.at[o], peer)
        copy.start()
        first_copies.append(copy)
    frecv[pl.ds(me, 1)] = fsend[pl.ds(me, 1)]
    for copy in first_copies:
        copy.wait_recv()
    total = frecv[0, 0:rows, :]
    for d in range(1, n):
        total = total + frecv[d, 0:rows, :]
    total = total * (1.0 / (n * E_DEV * SEQ))
    fred[0:rows, :] = total

    second_copies = []
    for o in range(1, n):
        peer = lax.rem(me + o, n)
        copy = to_dp(fred, fall.at[me], send2.at[o], recv2.at[o], peer)
        copy.start()
        second_copies.append(copy)
    fall[pl.ds(me, 1)] = fred[...][None]
    for copy in second_copies:
        copy.wait_recv()

    packed = jnp.concatenate([fall[d, 0:rows, :] for d in range(n)], axis=0)
    inverses = kron_inverses(packed, width)
    swapped = pltpu.roll(inverses, width, 1)
    inverse_a2 = jnp.where(first, inverses, swapped)
    inverse_g = swapped[:, :width]
    right = dot(tg_ref[...], inverse_a2, precision=HIGHEST)
    for e in range(E_DEV):
        span = slice(e * width, (e + 1) * width)
        flat_src[span, :] = dot(inverse_g, right[span], precision=HIGHEST)
    even = lax.broadcasted_iota(jnp.int32, (E_DEV, lanes), 1) < width
    per_chunk = chunk // lanes
    for m in range(width // 2):
        lo = flat_src[pl.ds(2 * m, E_DEV, stride=width), :]
        hi = flat_src[pl.ds(2 * m + 1, E_DEV, stride=width), :]
        c, at = m // per_chunk, (m % per_chunk) * lanes
        flat[c * E_DEV : (c + 1) * E_DEV, at : at + lanes] = jnp.where(even, lo, hi)
    tbuf[pl.ds(me, 1)] = flat[...].astype(jnp.bfloat16)[None]

    partner = me + 1 - 2 * lax.rem(me, 2)
    half = n // 2
    across = [to_dp(tbuf.at[me], tbuf.at[me], send_b.at[0], recv_b.at[0], partner)]
    along = []
    for o in range(1, half):
        peer = lax.rem(me + 2 * o, n)
        along.append(to_dp(tbuf.at[me], tbuf.at[me], send_a.at[o], recv_a.at[o], peer))
        along[-1].start()
    across[0].start()
    for o in range(1, half):
        source = lax.rem(me + n - 2 * o, n)
        to_dp(
            tbuf.at[source], tbuf.at[source], send_a.at[o], recv_a.at[o], partner
        ).wait_recv()
        across.append(
            to_dp(tbuf.at[source], tbuf.at[source], send_b.at[o], recv_b.at[o], partner)
        )
        across[-1].start()
    q_copy.wait()
    for o in range(half):
        source = lax.rem(partner + n - 2 * o, n)
        to_dp(
            tbuf.at[source], tbuf.at[source], send_b.at[o], recv_b.at[o], partner
        ).wait_recv()

    group = lax.broadcasted_iota(jnp.int32, (n * 16, owned), 0) % 16 // E_DEV
    got = jnp.zeros((n * 16, owned), jnp.float32)
    for c in range(chunks):
        queries = qbuf[:, c * chunk : (c + 1) * chunk]
        term = dot(tbuf[...].reshape(n * 16, chunk), queries, (1, 1))
        got = jnp.where(group == c, term, got)
    live_rows = []
    for d in range(n):
        tile = frecv[d, 8 * pl.cdiv(rows, 8) :, :][:, :owned]
        live_rows += [tile, tile]
    got = got * jnp.concatenate(live_rows, axis=0)
    out_lanes = part.shape[1]
    shape = (n * 16, out_lanes)
    src = lax.broadcasted_iota(jnp.int32, shape, 0)
    pick = (src // 16) * E_DEV + src % E_DEV == lax.broadcasted_iota(jnp.int32, shape, 1)
    scores = dot(got, pick.astype(jnp.float32), (0, 0), precision=HIGHEST)
    scale = 1.0 / float(width * width * layers) ** 0.5
    part[...] = scores * scale

    share = owned // layers
    last_copies = []
    for o in range(1, layers):
        peer = lax.rem(layer + o, layers)
        copy = pltpu.make_async_remote_copy(
            src_ref=part.at[pl.ds(pl.multiple_of(peer * share, 8), share)],
            dst_ref=sbuf.at[o],
            send_sem=send_s.at[o],
            recv_sem=recv_s.at[o],
            device_id=(me, peer),
            device_id_type=MESH,
        )
        copy.start()
        last_copies.append(copy)
    result = part[pl.ds(pl.multiple_of(layer * share, 8), share), :]
    for o, copy in enumerate(last_copies, 1):
        copy.wait_recv()
        result = result + sbuf[o]
    out_ref[...] = result[:, : out_ref.shape[1]]
    for copy in first_copies + second_copies + along + across + last_copies:
        copy.wait_send()


def body(x_act, g_out, proj_in, proj_out, queries, cand_ids, cand_counts):
    n = lax.axis_size("dp")
    layers = lax.axis_size("block")
    depth = x_act.shape[2]
    width = proj_in.shape[2]
    owned = queries.shape[1]
    rows = width // n
    pad = 8 * pl.cdiv(rows, 8)
    chunk = width * width * E_DEV // 16
    out_lanes = 128 * pl.cdiv(n * E_DEV, 128)
    bf16, f32 = jnp.bfloat16, jnp.float32
    sems = pltpu.SemaphoreType.DMA
    vmem = pltpu.VMEM
    return pl.pallas_call(
        functools.partial(kernel, n, layers),
        out_shape=jax.ShapeDtypeStruct((owned // layers, n * E_DEV), f32),
        in_specs=[pl.BlockSpec(memory_space=pltpu.HBM)] * 5
        + [pl.BlockSpec(memory_space=pltpu.SMEM)] * 2,
        out_specs=pl.BlockSpec(memory_space=pltpu.VMEM),
        scratch_shapes=[
            vmem((E_DEV, SEQ, depth), bf16),
            vmem((E_DEV, SEQ, depth), bf16),
            vmem((width, depth), bf16),
            vmem((width, depth), bf16),
            vmem((owned, width * width), bf16),
            vmem((n, pad + 8, 2 * width), f32),
            vmem((n, pad + 8, 2 * width), f32),
            vmem((pad, 2 * width), f32),
            vmem((n, pad, 2 * width), f32),
            vmem((E_DEV * width, width), f32),
            vmem((E_DEV * width, 2 * width), f32),
            vmem((16, chunk), f32),
            vmem((n, 16, chunk), bf16),
            vmem((owned, out_lanes), f32),
            vmem((layers, owned // layers, out_lanes), f32),
            sems((E_DEV,)),
            sems((E_DEV,)),
            sems((3,)),
            sems((n,)),
            sems((n,)),
            sems((n,)),
            sems((n,)),
            sems((n // 2,)),
            sems((n // 2,)),
            sems((n // 2,)),
            sems((n // 2,)),
            sems((layers,)),
            sems((layers,)),
        ],
        compiler_params=pltpu.CompilerParams(
            collective_id=0, has_side_effects=True, vmem_limit_bytes=40 * 1024 * 1024
        ),
        name="influence",
    )(
        x_act[0],
        g_out[0],
        jnp.swapaxes(proj_in, 1, 2)[0],
        jnp.swapaxes(proj_out, 1, 2)[0],
        queries[0],
        jnp.swapaxes(cand_ids, 1, 2)[0],
        cand_counts,
    )


def solution(mesh):
    return jax.shard_map(
        body,
        mesh=mesh,
        in_specs=(
            P("block", "dp", None),
            P("block", "dp", None),
            P("block", None, None),
            P("block", None, None),
            P("block", "dp", None),
            P("dp", None, None),
            P("dp", None),
        ),
        out_specs=P(("dp", "block"), None),
        check_vma=False,
    )
```

```python
import functools

import jax
import jax.numpy as jnp
from jax import lax
from jax.experimental import pallas as pl
from jax.experimental.pallas import tpu as pltpu
from jax.sharding import PartitionSpec as P

E_DEV = 4
SEQ = 128
QB = 4
CAP = 2
DAMP = 0.1
MESH = pl.DeviceIdType.MESH
HIGHEST = lax.Precision.HIGHEST


def dot(lhs, rhs, dims=(1, 0), precision=None):
    return lax.dot_general(
        lhs,
        rhs,
        (((dims[0],), (dims[1],)), ((), ())),
        preferred_element_type=jnp.float32,
        precision=precision,
    )


def kron_inverses(packed, width):
    shape = packed.shape
    lane_all = lax.broadcasted_iota(jnp.int32, shape, 1)
    first = lane_all < width
    lane = jnp.where(first, lane_all, lane_all - width)
    sub = lax.broadcasted_iota(jnp.int32, shape, 0)
    diag = jnp.sum(jnp.where(lane == sub, packed, 0.0), axis=0, keepdims=True)
    first_row = first[0:1]
    trace_a = jnp.sum(jnp.where(first_row, diag, 0.0), axis=1, keepdims=True)
    trace_g = jnp.sum(jnp.where(first_row, 0.0, diag), axis=1, keepdims=True)
    damping = DAMP * jnp.where(first_row, trace_a, trace_g) / width + 1e-06
    mat = packed + jnp.where(lane == sub, damping, 0.0)
    lane_row = lane[0:1]

    def column(k):
        col_a = jnp.broadcast_to(mat[:, k : k + 1], shape)
        col_g = jnp.broadcast_to(mat[:, width + k : width + k + 1], shape)
        return jnp.where(first, col_a, col_g)

    for k in range(0, width, 2):
        col0, col1 = column(k), column(k + 1)
        p00, p01, p11 = col0[k : k + 1], col0[k + 1 : k + 2], col1[k + 1 : k + 2]
        inv_det = 1.0 / (p00 * p11 - p01 * p01)
        at0, at1 = lane_row == k, lane_row == k + 1
        row0 = jnp.where(at0, 1.0, jnp.where(at1, 0.0, mat[k : k + 1]))
        row1 = jnp.where(at1, 1.0, jnp.where(at0, 0.0, mat[k + 1 : k + 2]))
        new0 = (p11 * row0 - p01 * row1) * inv_det
        new1 = (p00 * row1 - p01 * row0) * inv_det
        in0, in1 = sub == k, sub == k + 1
        keep = jnp.where((lane == k) | (lane == k + 1) | in0 | in1, 0.0, mat)
        mul0 = jnp.where(in0, -1.0, jnp.where(in1, 0.0, col0))
        mul1 = jnp.where(in1, -1.0, jnp.where(in0, 0.0, col1))
        mat = keep - mul0 * new0 - mul1 * new1
    return mat


def kernel(
    n, layers, x_hbm, g_hbm, pin_hbm, pout_hbm, q_hbm, ids_ref, counts_ref, out_ref,
    xbuf, gbuf, pin, pout, qbuf, fsend, frecv, fred, fall, tg_ref, flat_src, flat, tbuf,
    part, sbuf, load_x, load_g, load_p, send1, recv1, send2, recv2, send_a, recv_a,
    send_b, recv_b, send_s, recv_s,
):
    me = lax.axis_index("dp")
    layer = lax.axis_index("block")
    width = pin.shape[0]
    lanes = 2 * width
    owned = qbuf.shape[0]
    rows = width // n
    chunks = 16 // E_DEV
    chunk = tbuf.shape[2]

    loads = []
    pin_copy = pltpu.make_async_copy(pin_hbm, pin, load_p.at[0])
    pout_copy = pltpu.make_async_copy(pout_hbm, pout, load_p.at[1])
    q_copy = pltpu.make_async_copy(q_hbm, qbuf, load_p.at[2])
    pin_copy.start()
    pout_copy.start()
    for e in range(E_DEV):
        span = pl.ds(e * SEQ, SEQ)
        x_copy = pltpu.make_async_copy(x_hbm.at[span], xbuf.at[e], load_x.at[e])
        g_copy = pltpu.make_async_copy(g_hbm.at[span], gbuf.at[e], load_g.at[e])
        x_copy.start()
        g_copy.start()
        loads.append((x_copy, g_copy))
    q_copy.start()

    barrier = pltpu.get_barrier_semaphore()
    for o in range(1, n):
        pl.semaphore_signal(
            barrier, inc=1, device_id=(lax.rem(me + o, n), layer), device_id_type=MESH
        )
    for o in range(1, layers):
        pl.semaphore_signal(
            barrier, inc=1, device_id=(me, lax.rem(layer + o, layers)), device_id_type=MESH
        )

    lane_q = lax.broadcasted_iota(jnp.int32, (8, lanes), 1) // QB
    for p in range(n):
        live = jnp.zeros((8, lanes), jnp.float32)
        for s in range(CAP):
            wanted = jnp.where(s < counts_ref[0, p], ids_ref[s, p], -1)
            live = jnp.where(lane_q == wanted, 1.0, live)
        fsend[p, 8 * pl.cdiv(rows, 8) :, :] = live

    pin_copy.wait()
    pout_copy.wait()
    grams = jnp.zeros((lanes, lanes), jnp.float32)
    for e in range(E_DEV):
        loads[e][0].wait()
        act = dot(xbuf[e], pin[...], (1, 1))
        loads[e][1].wait()
        grad = dot(gbuf[e], pout[...], (1, 1))
        both = jnp.concatenate([act, grad], axis=1).astype(jnp.bfloat16)
        gram = dot(both, both, (0, 0))
        tg_ref[e * width : (e + 1) * width, :] = gram[width:, :width] * (1.0 / SEQ)
        grams = grams + gram
    lane_sq = lax.broadcasted_iota(jnp.int32, (width, lanes), 1)
    first = lane_sq < width
    factors = jnp.where(first, grams[:width], grams[width:])
    for p in range(n):
        fsend[p, 0:rows, :] = factors[p * rows : (p + 1) * rows]

    pl.semaphore_wait(barrier, n - 1 + layers - 1)

    def to_dp(src, dst, send, recv, peer):
        return pltpu.make_async_remote_copy(
            src_ref=src, dst_ref=dst, send_sem=send, recv_sem=recv,
            device_id=(peer, layer), device_id_type=MESH,
        )

    first_copies = []
    for o in range(1, n):
        peer = lax.rem(me + o, n)
        copy = to_dp(fsend.at[peer], frecv.at[me], send1.at[o], recv1.at[o], peer)
        copy.start()
        first_copies.append(copy)
    frecv[pl.ds(me, 1)] = fsend[pl.ds(me, 1)]
    for copy in first_copies:
        copy.wait_recv()
    total = frecv[0, 0:rows, :]
    for d in range(1, n):
        total = total + frecv[d, 0:rows, :]
    total = total * (1.0 / (n * E_DEV * SEQ))
    fred[0:rows, :] = total

    second_copies = []
    for o in range(1, n):
        peer = lax.rem(me + o, n)
        copy = to_dp(fred, fall.at[me], send2.at[o], recv2.at[o], peer)
        copy.start()
        second_copies.append(copy)
    fall[pl.ds(me, 1)] = fred[...][None]
    for copy in second_copies:
        copy.wait_recv()

    packed = jnp.concatenate([fall[d, 0:rows, :] for d in range(n)], axis=0)
    inverses = kron_inverses(packed, width)
    swapped = pltpu.roll(inverses, width, 1)
    inverse_a2 = jnp.where(first, inverses, swapped)
    inverse_g = swapped[:, :width]
    right = dot(tg_ref[...], inverse_a2, precision=HIGHEST)
    for e in range(E_DEV):
        span = slice(e * width, (e + 1) * width)
        flat_src[span, :] = dot(inverse_g, right[span], precision=HIGHEST)
    even = lax.broadcasted_iota(jnp.int32, (E_DEV, lanes), 1) < width
    per_chunk = chunk // lanes
    for m in range(width // 2):
        lo = flat_src[pl.ds(2 * m, E_DEV, stride=width), :]
        hi = flat_src[pl.ds(2 * m + 1, E_DEV, stride=width), :]
        c, at = m // per_chunk, (m % per_chunk) * lanes
        flat[c * E_DEV : (c + 1) * E_DEV, at : at + lanes] = jnp.where(even, lo, hi)
    tbuf[pl.ds(me, 1)] = flat[...].astype(jnp.bfloat16)[None]

    partner = me + 1 - 2 * lax.rem(me, 2)
    half = n // 2
    across = [to_dp(tbuf.at[me], tbuf.at[me], send_b.at[0], recv_b.at[0], partner)]
    along = []
    for o in range(1, half):
        peer = lax.rem(me + 2 * o, n)
        along.append(to_dp(tbuf.at[me], tbuf.at[me], send_a.at[o], recv_a.at[o], peer))
        along[-1].start()
    across[0].start()
    for o in range(1, half):
        source = lax.rem(me + n - 2 * o, n)
        to_dp(
            tbuf.at[source], tbuf.at[source], send_a.at[o], recv_a.at[o], partner
        ).wait_recv()
        across.append(
            to_dp(tbuf.at[source], tbuf.at[source], send_b.at[o], recv_b.at[o], partner)
        )
        across[-1].start()
    q_copy.wait()
    for o in range(half):
        source = lax.rem(partner + n - 2 * o, n)
        to_dp(
            tbuf.at[source], tbuf.at[source], send_b.at[o], recv_b.at[o], partner
        ).wait_recv()

    group = lax.broadcasted_iota(jnp.int32, (n * 16, owned), 0) % 16 // E_DEV
    got = jnp.zeros((n * 16, owned), jnp.float32)
    for c in range(chunks):
        queries = qbuf[:, c * chunk : (c + 1) * chunk]
        term = dot(tbuf[...].reshape(n * 16, chunk), queries, (1, 1))
        got = jnp.where(group == c, term, got)
    live_rows = []
    for d in range(n):
        tile = frecv[d, 8 * pl.cdiv(rows, 8) :, :][:, :owned]
        live_rows += [tile, tile]
    got = got * jnp.concatenate(live_rows, axis=0)
    out_lanes = part.shape[1]
    shape = (n * 16, out_lanes)
    src = lax.broadcasted_iota(jnp.int32, shape, 0)
    pick = (src // 16) * E_DEV + src % E_DEV == lax.broadcasted_iota(jnp.int32, shape, 1)
    scores = dot(got, pick.astype(jnp.float32), (0, 0), precision=HIGHEST)
    scale = 1.0 / float(width * width * layers) ** 0.5
    part[...] = scores * scale

    share = owned // layers
    last_copies = []
    for o in range(1, layers):
        peer = lax.rem(layer + o, layers)
        copy = pltpu.make_async_remote_copy(
            src_ref=part.at[pl.ds(pl.multiple_of(peer * share, 8), share)],
            dst_ref=sbuf.at[o],
            send_sem=send_s.at[o],
            recv_sem=recv_s.at[o],
            device_id=(me, peer),
            device_id_type=MESH,
        )
        copy.start()
        last_copies.append(copy)
    result = part[pl.ds(pl.multiple_of(layer * share, 8), share), :]
    for o, copy in enumerate(last_copies, 1):
        copy.wait_recv()
        result = result + sbuf[o]
    out_ref[...] = result[:, : out_ref.shape[1]]
    for copy in first_copies + second_copies + along + across + last_copies:
        copy.wait_send()


def body(x_act, g_out, proj_in, proj_out, queries, cand_ids, cand_counts):
    n = lax.axis_size("dp")
    layers = lax.axis_size("block")
    depth = x_act.shape[2]
    width = proj_in.shape[2]
    owned = queries.shape[1]
    rows = width // n
    pad = 8 * pl.cdiv(rows, 8)
    chunk = width * width * E_DEV // 16
    out_lanes = 128 * pl.cdiv(n * E_DEV, 128)
    bf16, f32 = jnp.bfloat16, jnp.float32
    sems = pltpu.SemaphoreType.DMA
    vmem = pltpu.VMEM
    return pl.pallas_call(
        functools.partial(kernel, n, layers),
        out_shape=jax.ShapeDtypeStruct((owned // layers, n * E_DEV), f32),
        in_specs=[pl.BlockSpec(memory_space=pltpu.HBM)] * 5
        + [pl.BlockSpec(memory_space=pltpu.SMEM)] * 2,
        out_specs=pl.BlockSpec(memory_space=pltpu.VMEM),
        scratch_shapes=[
            vmem((E_DEV, SEQ, depth), bf16),
            vmem((E_DEV, SEQ, depth), bf16),
            vmem((width, depth), bf16),
            vmem((width, depth), bf16),
            vmem((owned, width * width), bf16),
            vmem((n, pad + 8, 2 * width), f32),
            vmem((n, pad + 8, 2 * width), f32),
            vmem((pad, 2 * width), f32),
            vmem((n, pad, 2 * width), f32),
            vmem((E_DEV * width, width), f32),
            vmem((E_DEV * width, 2 * width), f32),
            vmem((16, chunk), f32),
            vmem((n, 16, chunk), bf16),
            vmem((owned, out_lanes), f32),
            vmem((layers, owned // layers, out_lanes), f32),
            sems((E_DEV,)),
            sems((E_DEV,)),
            sems((3,)),
            sems((n,)),
            sems((n,)),
            sems((n,)),
            sems((n,)),
            sems((n // 2,)),
            sems((n // 2,)),
            sems((n // 2,)),
            sems((n // 2,)),
            sems((layers,)),
            sems((layers,)),
        ],
        compiler_params=pltpu.CompilerParams(
            collective_id=0, has_side_effects=True, vmem_limit_bytes=64 * 1024 * 1024 - 131072
        ),
        name="influence",
    )(
        x_act[0],
        g_out[0],
        jnp.swapaxes(proj_in, 1, 2)[0],
        jnp.swapaxes(proj_out, 1, 2)[0],
        queries[0],
        jnp.swapaxes(cand_ids, 1, 2)[0],
        cand_counts,
    )


def solution(mesh):
    return jax.shard_map(
        body,
        mesh=mesh,
        in_specs=(
            P("block", "dp", None),
            P("block", "dp", None),
            P("block", None, None),
            P("block", None, None),
            P("block", "dp", None),
            P("dp", None, None),
            P("dp", None),
        ),
        out_specs=P(("dp", "block"), None),
        check_vma=False,
    )
```

```python
import functools

import jax
import jax.numpy as jnp
from jax import lax
from jax.experimental import pallas as pl
from jax.experimental.pallas import tpu as pltpu
from jax.sharding import PartitionSpec as P

E_DEV = 4
SEQ = 128
QB = 4
CAP = 2
DAMP = 0.1
MESH = pl.DeviceIdType.MESH
HIGHEST = lax.Precision.HIGHEST


def dot(lhs, rhs, dims=(1, 0), precision=None):
    return lax.dot_general(
        lhs,
        rhs,
        (((dims[0],), (dims[1],)), ((), ())),
        preferred_element_type=jnp.float32,
        precision=precision,
    )


def kron_inverses(packed, width):
    shape = packed.shape
    lane_all = lax.broadcasted_iota(jnp.int32, shape, 1)
    first = lane_all < width
    lane = jnp.where(first, lane_all, lane_all - width)
    sub = lax.broadcasted_iota(jnp.int32, shape, 0)
    diag = jnp.sum(jnp.where(lane == sub, packed, 0.0), axis=0, keepdims=True)
    first_row = first[0:1]
    trace_a = jnp.sum(jnp.where(first_row, diag, 0.0), axis=1, keepdims=True)
    trace_g = jnp.sum(jnp.where(first_row, 0.0, diag), axis=1, keepdims=True)
    damping = DAMP * jnp.where(first_row, trace_a, trace_g) / width + 1e-06
    mat = packed + jnp.where(lane == sub, damping, 0.0)
    lane_row = lane[0:1]

    def column(k):
        col_a = jnp.broadcast_to(mat[:, k : k + 1], shape)
        col_g = jnp.broadcast_to(mat[:, width + k : width + k + 1], shape)
        return jnp.where(first, col_a, col_g)

    col0, col1 = column(0), column(1)
    for k in range(0, width, 2):
        after = [j for j in (k + 2, k + 3) if j < width]
        stale = [column(j) for j in after]
        p00, p01, p11 = col0[k : k + 1], col0[k + 1 : k + 2], col1[k + 1 : k + 2]
        inv_det = 1.0 / (p00 * p11 - p01 * p01)
        at0, at1 = lane_row == k, lane_row == k + 1
        row0 = jnp.where(at0, 1.0, jnp.where(at1, 0.0, mat[k : k + 1]))
        row1 = jnp.where(at1, 1.0, jnp.where(at0, 0.0, mat[k + 1 : k + 2]))
        new0 = (p11 * row0 - p01 * row1) * inv_det
        new1 = (p00 * row1 - p01 * row0) * inv_det
        in0, in1 = sub == k, sub == k + 1
        keep = jnp.where((lane == k) | (lane == k + 1) | in0 | in1, 0.0, mat)
        mul0 = jnp.where(in0, -1.0, jnp.where(in1, 0.0, col0))
        mul1 = jnp.where(in1, -1.0, jnp.where(in0, 0.0, col1))
        fresh = []
        for j, old in zip(after, stale):
            c0, c1 = col0[j : j + 1], col1[j : j + 1]
            n0 = (p11 * c0 - p01 * c1) * inv_det
            n1 = (p00 * c1 - p01 * c0) * inv_det
            fresh.append(jnp.where(in0 | in1, 0.0, old) - mul0 * n0 - mul1 * n1)
        mat = keep - mul0 * new0 - mul1 * new1
        if fresh:
            col0, col1 = fresh
    return mat


def kernel(
    n, layers, x_hbm, g_hbm, pin_hbm, pout_hbm, q_hbm, ids_ref, counts_ref, out_ref,
    xbuf, gbuf, pin, pout, qbuf, fsend, frecv, fred, fall, tg_ref, flat_src, flat, tbuf,
    part, sbuf, load_x, load_g, load_p, send1, recv1, send2, recv2, send_a, recv_a,
    send_b, recv_b, send_s, recv_s,
):
    me = lax.axis_index("dp")
    layer = lax.axis_index("block")
    width = pin.shape[0]
    lanes = 2 * width
    owned = qbuf.shape[0]
    rows = width // n
    chunks = 16 // E_DEV
    chunk = tbuf.shape[2]

    loads = []
    pin_copy = pltpu.make_async_copy(pin_hbm, pin, load_p.at[0])
    pout_copy = pltpu.make_async_copy(pout_hbm, pout, load_p.at[1])
    q_copy = pltpu.make_async_copy(q_hbm, qbuf, load_p.at[2])
    pin_copy.start()
    pout_copy.start()
    for e in range(E_DEV):
        span = pl.ds(e * SEQ, SEQ)
        x_copy = pltpu.make_async_copy(x_hbm.at[span], xbuf.at[e], load_x.at[e])
        g_copy = pltpu.make_async_copy(g_hbm.at[span], gbuf.at[e], load_g.at[e])
        x_copy.start()
        g_copy.start()
        loads.append((x_copy, g_copy))
    q_copy.start()

    barrier = pltpu.get_barrier_semaphore()
    for o in range(1, n):
        pl.semaphore_signal(
            barrier, inc=1, device_id=(lax.rem(me + o, n), layer), device_id_type=MESH
        )
    for o in range(1, layers):
        pl.semaphore_signal(
            barrier, inc=1, device_id=(me, lax.rem(layer + o, layers)), device_id_type=MESH
        )

    lane_q = lax.broadcasted_iota(jnp.int32, (8, lanes), 1) // QB
    for p in range(n):
        live = jnp.zeros((8, lanes), jnp.float32)
        for s in range(CAP):
            wanted = jnp.where(s < counts_ref[0, p], ids_ref[s, p], -1)
            live = jnp.where(lane_q == wanted, 1.0, live)
        fsend[p, 8 * pl.cdiv(rows, 8) :, :] = live

    pin_copy.wait()
    pout_copy.wait()
    grams = jnp.zeros((lanes, lanes), jnp.float32)
    for e in range(E_DEV):
        loads[e][0].wait()
        act = dot(xbuf[e], pin[...], (1, 1))
        loads[e][1].wait()
        grad = dot(gbuf[e], pout[...], (1, 1))
        both = jnp.concatenate([act, grad], axis=1).astype(jnp.bfloat16)
        gram = dot(both, both, (0, 0))
        tg_ref[e * width : (e + 1) * width, :] = gram[width:, :width] * (1.0 / SEQ)
        grams = grams + gram
    lane_sq = lax.broadcasted_iota(jnp.int32, (width, lanes), 1)
    first = lane_sq < width
    factors = jnp.where(first, grams[:width], grams[width:])
    for p in range(n):
        fsend[p, 0:rows, :] = factors[p * rows : (p + 1) * rows]

    pl.semaphore_wait(barrier, n - 1 + layers - 1)

    def to_dp(src, dst, send, recv, peer):
        return pltpu.make_async_remote_copy(
            src_ref=src, dst_ref=dst, send_sem=send, recv_sem=recv,
            device_id=(peer, layer), device_id_type=MESH,
        )

    first_copies = []
    for o in range(1, n):
        peer = lax.rem(me + o, n)
        copy = to_dp(fsend.at[peer], frecv.at[me], send1.at[o], recv1.at[o], peer)
        copy.start()
        first_copies.append(copy)
    frecv[pl.ds(me, 1)] = fsend[pl.ds(me, 1)]
    for copy in first_copies:
        copy.wait_recv()
    total = frecv[0, 0:rows, :]
    for d in range(1, n):
        total = total + frecv[d, 0:rows, :]
    total = total * (1.0 / (n * E_DEV * SEQ))
    fred[0:rows, :] = total

    second_copies = []
    for o in range(1, n):
        peer = lax.rem(me + o, n)
        copy = to_dp(fred, fall.at[me], send2.at[o], recv2.at[o], peer)
        copy.start()
        second_copies.append(copy)
    fall[pl.ds(me, 1)] = fred[...][None]
    for copy in second_copies:
        copy.wait_recv()

    packed = jnp.concatenate([fall[d, 0:rows, :] for d in range(n)], axis=0)
    inverses = kron_inverses(packed, width)
    swapped = pltpu.roll(inverses, width, 1)
    inverse_a2 = jnp.where(first, inverses, swapped)
    inverse_g = swapped[:, :width]
    right = dot(tg_ref[...], inverse_a2, precision=HIGHEST)
    for e in range(E_DEV):
        span = slice(e * width, (e + 1) * width)
        flat_src[span, :] = dot(inverse_g, right[span], precision=HIGHEST)
    even = lax.broadcasted_iota(jnp.int32, (E_DEV, lanes), 1) < width
    per_chunk = chunk // lanes
    for m in range(width // 2):
        lo = flat_src[pl.ds(2 * m, E_DEV, stride=width), :]
        hi = flat_src[pl.ds(2 * m + 1, E_DEV, stride=width), :]
        c, at = m // per_chunk, (m % per_chunk) * lanes
        flat[c * E_DEV : (c + 1) * E_DEV, at : at + lanes] = jnp.where(even, lo, hi)
    tbuf[pl.ds(me, 1)] = flat[...].astype(jnp.bfloat16)[None]

    partner = me + 1 - 2 * lax.rem(me, 2)
    half = n // 2
    across = [to_dp(tbuf.at[me], tbuf.at[me], send_b.at[0], recv_b.at[0], partner)]
    along = []
    for o in range(1, half):
        peer = lax.rem(me + 2 * o, n)
        along.append(to_dp(tbuf.at[me], tbuf.at[me], send_a.at[o], recv_a.at[o], peer))
        along[-1].start()
    across[0].start()
    for o in range(1, half):
        source = lax.rem(me + n - 2 * o, n)
        to_dp(
            tbuf.at[source], tbuf.at[source], send_a.at[o], recv_a.at[o], partner
        ).wait_recv()
        across.append(
            to_dp(tbuf.at[source], tbuf.at[source], send_b.at[o], recv_b.at[o], partner)
        )
        across[-1].start()
    q_copy.wait()
    for o in range(half):
        source = lax.rem(partner + n - 2 * o, n)
        to_dp(
            tbuf.at[source], tbuf.at[source], send_b.at[o], recv_b.at[o], partner
        ).wait_recv()

    group = lax.broadcasted_iota(jnp.int32, (n * 16, owned), 0) % 16 // E_DEV
    got = jnp.zeros((n * 16, owned), jnp.float32)
    for c in range(chunks):
        queries = qbuf[:, c * chunk : (c + 1) * chunk]
        term = dot(tbuf[...].reshape(n * 16, chunk), queries, (1, 1))
        got = jnp.where(group == c, term, got)
    live_rows = []
    for d in range(n):
        tile = frecv[d, 8 * pl.cdiv(rows, 8) :, :][:, :owned]
        live_rows += [tile, tile]
    got = got * jnp.concatenate(live_rows, axis=0)
    out_lanes = part.shape[1]
    shape = (n * 16, out_lanes)
    src = lax.broadcasted_iota(jnp.int32, shape, 0)
    pick = (src // 16) * E_DEV + src % E_DEV == lax.broadcasted_iota(jnp.int32, shape, 1)
    scores = dot(got, pick.astype(jnp.float32), (0, 0), precision=HIGHEST)
    scale = 1.0 / float(width * width * layers) ** 0.5
    part[...] = scores * scale

    share = owned // layers
    last_copies = []
    for o in range(1, layers):
        peer = lax.rem(layer + o, layers)
        copy = pltpu.make_async_remote_copy(
            src_ref=part.at[pl.ds(pl.multiple_of(peer * share, 8), share)],
            dst_ref=sbuf.at[o],
            send_sem=send_s.at[o],
            recv_sem=recv_s.at[o],
            device_id=(me, peer),
            device_id_type=MESH,
        )
        copy.start()
        last_copies.append(copy)
    result = part[pl.ds(pl.multiple_of(layer * share, 8), share), :]
    for o, copy in enumerate(last_copies, 1):
        copy.wait_recv()
        result = result + sbuf[o]
    out_ref[...] = result[:, : out_ref.shape[1]]
    for copy in first_copies + second_copies + along + across + last_copies:
        copy.wait_send()


def body(x_act, g_out, proj_in, proj_out, queries, cand_ids, cand_counts):
    n = lax.axis_size("dp")
    layers = lax.axis_size("block")
    depth = x_act.shape[2]
    width = proj_in.shape[2]
    owned = queries.shape[1]
    rows = width // n
    pad = 8 * pl.cdiv(rows, 8)
    chunk = width * width * E_DEV // 16
    out_lanes = 128 * pl.cdiv(n * E_DEV, 128)
    bf16, f32 = jnp.bfloat16, jnp.float32
    sems = pltpu.SemaphoreType.DMA
    vmem = pltpu.VMEM
    return pl.pallas_call(
        functools.partial(kernel, n, layers),
        out_shape=jax.ShapeDtypeStruct((owned // layers, n * E_DEV), f32),
        in_specs=[pl.BlockSpec(memory_space=pltpu.HBM)] * 5
        + [pl.BlockSpec(memory_space=pltpu.SMEM)] * 2,
        out_specs=pl.BlockSpec(memory_space=pltpu.VMEM),
        scratch_shapes=[
            vmem((E_DEV, SEQ, depth), bf16),
            vmem((E_DEV, SEQ, depth), bf16),
            vmem((width, depth), bf16),
            vmem((width, depth), bf16),
            vmem((owned, width * width), bf16),
            vmem((n, pad + 8, 2 * width), f32),
            vmem((n, pad + 8, 2 * width), f32),
            vmem((pad, 2 * width), f32),
            vmem((n, pad, 2 * width), f32),
            vmem((E_DEV * width, width), f32),
            vmem((E_DEV * width, 2 * width), f32),
            vmem((16, chunk), f32),
            vmem((n, 16, chunk), bf16),
            vmem((owned, out_lanes), f32),
            vmem((layers, owned // layers, out_lanes), f32),
            sems((E_DEV,)),
            sems((E_DEV,)),
            sems((3,)),
            sems((n,)),
            sems((n,)),
            sems((n,)),
            sems((n,)),
            sems((n // 2,)),
            sems((n // 2,)),
            sems((n // 2,)),
            sems((n // 2,)),
            sems((layers,)),
            sems((layers,)),
        ],
        compiler_params=pltpu.CompilerParams(
            collective_id=0, has_side_effects=True, vmem_limit_bytes=64 * 1024 * 1024 - 131072
        ),
        name="influence",
    )(
        x_act[0],
        g_out[0],
        jnp.swapaxes(proj_in, 1, 2)[0],
        jnp.swapaxes(proj_out, 1, 2)[0],
        queries[0],
        jnp.swapaxes(cand_ids, 1, 2)[0],
        cand_counts,
    )


def solution(mesh):
    return jax.shard_map(
        body,
        mesh=mesh,
        in_specs=(
            P("block", "dp", None),
            P("block", "dp", None),
            P("block", None, None),
            P("block", None, None),
            P("block", "dp", None),
            P("dp", None, None),
            P("dp", None),
        ),
        out_specs=P(("dp", "block"), None),
        check_vma=False,
    )
```

```python
import functools

import jax
import jax.numpy as jnp
from jax import lax
from jax.experimental import pallas as pl
from jax.experimental.pallas import tpu as pltpu
from jax.sharding import PartitionSpec as P

E_DEV = 4
SEQ = 128
QB = 4
CAP = 2
DAMP = 0.1
MESH = pl.DeviceIdType.MESH
HIGHEST = lax.Precision.HIGHEST


def dot(lhs, rhs, dims=(1, 0), precision=None):
    return lax.dot_general(
        lhs,
        rhs,
        (((dims[0],), (dims[1],)), ((), ())),
        preferred_element_type=jnp.float32,
        precision=precision,
    )


def kron_inverses(packed, width):
    shape = packed.shape
    lane_all = lax.broadcasted_iota(jnp.int32, shape, 1)
    first = lane_all < width
    lane = jnp.where(first, lane_all, lane_all - width)
    sub = lax.broadcasted_iota(jnp.int32, shape, 0)
    diag = jnp.sum(jnp.where(lane == sub, packed, 0.0), axis=0, keepdims=True)
    first_row = first[0:1]
    trace_a = jnp.sum(jnp.where(first_row, diag, 0.0), axis=1, keepdims=True)
    trace_g = jnp.sum(jnp.where(first_row, 0.0, diag), axis=1, keepdims=True)
    damping = DAMP * jnp.where(first_row, trace_a, trace_g) / width + 1e-06
    mat = packed + jnp.where(lane == sub, damping, 0.0)
    lane_row = lane[0:1]

    def column(k):
        col_a = jnp.broadcast_to(mat[:, k : k + 1], shape)
        col_g = jnp.broadcast_to(mat[:, width + k : width + k + 1], shape)
        return jnp.where(first, col_a, col_g)

    col0, col1 = column(0), column(1)
    for k in range(0, width, 2):
        after = [j for j in (k + 2, k + 3) if j < width]
        stale = [column(j) for j in after]
        p00, p01, p11 = col0[k : k + 1], col0[k + 1 : k + 2], col1[k + 1 : k + 2]
        inv_det = 1.0 / (p00 * p11 - p01 * p01)
        at0, at1 = lane_row == k, lane_row == k + 1
        row0 = jnp.where(at0, 1.0, jnp.where(at1, 0.0, mat[k : k + 1]))
        row1 = jnp.where(at1, 1.0, jnp.where(at0, 0.0, mat[k + 1 : k + 2]))
        new0 = (p11 * row0 - p01 * row1) * inv_det
        new1 = (p00 * row1 - p01 * row0) * inv_det
        in0, in1 = sub == k, sub == k + 1
        keep = jnp.where((lane == k) | (lane == k + 1) | in0 | in1, 0.0, mat)
        mul0 = jnp.where(in0, -1.0, jnp.where(in1, 0.0, col0))
        mul1 = jnp.where(in1, -1.0, jnp.where(in0, 0.0, col1))
        fresh = []
        for j, old in zip(after, stale):
            c0, c1 = col0[j : j + 1], col1[j : j + 1]
            n0 = (p11 * c0 - p01 * c1) * inv_det
            n1 = (p00 * c1 - p01 * c0) * inv_det
            fresh.append(jnp.where(in0 | in1, 0.0, old) - mul0 * n0 - mul1 * n1)
        mat = keep - mul0 * new0 - mul1 * new1
        if fresh:
            col0, col1 = fresh
    return mat


def kernel(
    n, layers, x_hbm, g_hbm, pin_hbm, pout_hbm, q_hbm, ids_ref, counts_ref, out_ref,
    xbuf, gbuf, pin, pout, qbuf, fsend, frecv, fred, fall, tg_ref, flat_src, flat, tbuf,
    part, sbuf, load_x, load_g, load_p, send1, recv1, send2, recv2, send_a, recv_a,
    send_b, recv_b, send_s, recv_s,
):
    me = lax.axis_index("dp")
    layer = lax.axis_index("block")
    width = pin.shape[0]
    lanes = 2 * width
    owned = qbuf.shape[0]
    rows = width // n
    chunks = 16 // E_DEV
    chunk = tbuf.shape[2]

    loads = []
    pin_copy = pltpu.make_async_copy(pin_hbm, pin, load_p.at[0])
    pout_copy = pltpu.make_async_copy(pout_hbm, pout, load_p.at[1])
    q_copy = pltpu.make_async_copy(q_hbm, qbuf, load_p.at[2])
    pin_copy.start()
    pout_copy.start()
    for e in range(E_DEV):
        span = pl.ds(e * SEQ, SEQ)
        x_copy = pltpu.make_async_copy(x_hbm.at[span], xbuf.at[e], load_x.at[e])
        g_copy = pltpu.make_async_copy(g_hbm.at[span], gbuf.at[e], load_g.at[e])
        x_copy.start()
        g_copy.start()
        loads.append((x_copy, g_copy))
    q_copy.start()

    barrier = pltpu.get_barrier_semaphore()
    for o in range(1, n):
        pl.semaphore_signal(
            barrier, inc=1, device_id=(lax.rem(me + o, n), layer), device_id_type=MESH
        )
    for o in range(1, layers):
        pl.semaphore_signal(
            barrier, inc=1, device_id=(me, lax.rem(layer + o, layers)), device_id_type=MESH
        )

    lane_q = lax.broadcasted_iota(jnp.int32, (8, lanes), 1) // QB
    for p in range(n):
        live = jnp.zeros((8, lanes), jnp.float32)
        for s in range(CAP):
            wanted = jnp.where(s < counts_ref[0, p], ids_ref[s, p], -1)
            live = jnp.where(lane_q == wanted, 1.0, live)
        fsend[p, 8 * pl.cdiv(rows, 8) :, :] = live

    pin_copy.wait()
    pout_copy.wait()
    grams = jnp.zeros((lanes, lanes), jnp.float32)
    for e in range(E_DEV):
        loads[e][0].wait()
        act = dot(xbuf[e], pin[...], (1, 1))
        loads[e][1].wait()
        grad = dot(gbuf[e], pout[...], (1, 1))
        both = jnp.concatenate([act, grad], axis=1).astype(jnp.bfloat16)
        gram = dot(both, both, (0, 0))
        tg_ref[e * width : (e + 1) * width, :] = gram[width:, :width] * (1.0 / SEQ)
        grams = grams + gram
    lane_sq = lax.broadcasted_iota(jnp.int32, (width, lanes), 1)
    first = lane_sq < width
    factors = jnp.where(first, grams[:width], grams[width:])
    for p in range(n):
        fsend[p, 0:rows, :] = factors[p * rows : (p + 1) * rows]

    pl.semaphore_wait(barrier, n - 1 + layers - 1)

    def to_dp(src, dst, send, recv, peer):
        return pltpu.make_async_remote_copy(
            src_ref=src, dst_ref=dst, send_sem=send, recv_sem=recv,
            device_id=(peer, layer), device_id_type=MESH,
        )

    first_copies = []
    for o in range(1, n):
        peer = lax.rem(me + o, n)
        copy = to_dp(fsend.at[peer], frecv.at[me], send1.at[o], recv1.at[o], peer)
        copy.start()
        first_copies.append(copy)
    frecv[pl.ds(me, 1)] = fsend[pl.ds(me, 1)]
    for copy in first_copies:
        copy.wait_recv()
    total = frecv[0, 0:rows, :]
    for d in range(1, n):
        total = total + frecv[d, 0:rows, :]
    total = total * (1.0 / (n * E_DEV * SEQ))
    fred[0:rows, :] = total

    second_copies = []
    for o in range(1, n):
        peer = lax.rem(me + o, n)
        copy = to_dp(fred, fall.at[me], send2.at[o], recv2.at[o], peer)
        copy.start()
        second_copies.append(copy)
    fall[pl.ds(me, 1)] = fred[...][None]
    for copy in second_copies:
        copy.wait_recv()

    packed = jnp.concatenate([fall[d, 0:rows, :] for d in range(n)], axis=0)
    inverses = kron_inverses(packed, width)
    swapped = pltpu.roll(inverses, width, 1)
    inverse_a2 = jnp.where(first, inverses, swapped)
    inverse_g = swapped[:, :width]
    right = dot(tg_ref[...], inverse_a2, precision=HIGHEST)
    for e in range(E_DEV):
        span = slice(e * width, (e + 1) * width)
        flat_src[span, :] = dot(inverse_g, right[span], precision=HIGHEST)
    even = lax.broadcasted_iota(jnp.int32, (E_DEV, lanes), 1) < width
    per_chunk = chunk // lanes
    for m in range(width // 2):
        lo = flat_src[pl.ds(2 * m, E_DEV, stride=width), :]
        hi = flat_src[pl.ds(2 * m + 1, E_DEV, stride=width), :]
        c, at = m // per_chunk, (m % per_chunk) * lanes
        flat[c * E_DEV : (c + 1) * E_DEV, at : at + lanes] = jnp.where(even, lo, hi)
    tbuf[pl.ds(me, 1)] = flat[...].astype(jnp.bfloat16)[None]

    partner = me + 1 - 2 * lax.rem(me, 2)
    half = n // 2
    across, along = [], []
    for o in range(1, half):
        peer = lax.rem(me + 2 * o, n)
        along.append(to_dp(tbuf.at[me], tbuf.at[me], send_a.at[o], recv_a.at[o], peer))
        along[-1].start()
    for o in range(half):
        peer = lax.rem(partner + 2 * o, n)
        across.append(to_dp(tbuf.at[me], tbuf.at[me], send_b.at[o], recv_b.at[o], peer))
        across[-1].start()
    for o in range(1, half):
        source = lax.rem(me + n - 2 * o, n)
        to_dp(
            tbuf.at[source], tbuf.at[source], send_a.at[o], recv_a.at[o], partner
        ).wait_recv()
    q_copy.wait()
    for o in range(half):
        source = lax.rem(partner + n - 2 * o, n)
        to_dp(
            tbuf.at[source], tbuf.at[source], send_b.at[o], recv_b.at[o], partner
        ).wait_recv()

    group = lax.broadcasted_iota(jnp.int32, (n * 16, owned), 0) % 16 // E_DEV
    got = jnp.zeros((n * 16, owned), jnp.float32)
    for c in range(chunks):
        queries = qbuf[:, c * chunk : (c + 1) * chunk]
        term = dot(tbuf[...].reshape(n * 16, chunk), queries, (1, 1))
        got = jnp.where(group == c, term, got)
    live_rows = []
    for d in range(n):
        tile = frecv[d, 8 * pl.cdiv(rows, 8) :, :][:, :owned]
        live_rows += [tile, tile]
    got = got * jnp.concatenate(live_rows, axis=0)
    out_lanes = part.shape[1]
    shape = (n * 16, out_lanes)
    src = lax.broadcasted_iota(jnp.int32, shape, 0)
    pick = (src // 16) * E_DEV + src % E_DEV == lax.broadcasted_iota(jnp.int32, shape, 1)
    scores = dot(got, pick.astype(jnp.float32), (0, 0), precision=HIGHEST)
    scale = 1.0 / float(width * width * layers) ** 0.5
    part[...] = scores * scale

    share = owned // layers
    last_copies = []
    for o in range(1, layers):
        peer = lax.rem(layer + o, layers)
        copy = pltpu.make_async_remote_copy(
            src_ref=part.at[pl.ds(pl.multiple_of(peer * share, 8), share)],
            dst_ref=sbuf.at[o],
            send_sem=send_s.at[o],
            recv_sem=recv_s.at[o],
            device_id=(me, peer),
            device_id_type=MESH,
        )
        copy.start()
        last_copies.append(copy)
    result = part[pl.ds(pl.multiple_of(layer * share, 8), share), :]
    for o, copy in enumerate(last_copies, 1):
        copy.wait_recv()
        result = result + sbuf[o]
    out_ref[...] = result[:, : out_ref.shape[1]]
    for copy in first_copies + second_copies + along + across + last_copies:
        copy.wait_send()


def body(x_act, g_out, proj_in, proj_out, queries, cand_ids, cand_counts):
    n = lax.axis_size("dp")
    layers = lax.axis_size("block")
    depth = x_act.shape[2]
    width = proj_in.shape[2]
    owned = queries.shape[1]
    rows = width // n
    pad = 8 * pl.cdiv(rows, 8)
    chunk = width * width * E_DEV // 16
    out_lanes = 128 * pl.cdiv(n * E_DEV, 128)
    bf16, f32 = jnp.bfloat16, jnp.float32
    sems = pltpu.SemaphoreType.DMA
    vmem = pltpu.VMEM
    return pl.pallas_call(
        functools.partial(kernel, n, layers),
        out_shape=jax.ShapeDtypeStruct((owned // layers, n * E_DEV), f32),
        in_specs=[pl.BlockSpec(memory_space=pltpu.HBM)] * 5
        + [pl.BlockSpec(memory_space=pltpu.SMEM)] * 2,
        out_specs=pl.BlockSpec(memory_space=pltpu.VMEM),
        scratch_shapes=[
            vmem((E_DEV, SEQ, depth), bf16),
            vmem((E_DEV, SEQ, depth), bf16),
            vmem((width, depth), bf16),
            vmem((width, depth), bf16),
            vmem((owned, width * width), bf16),
            vmem((n, pad + 8, 2 * width), f32),
            vmem((n, pad + 8, 2 * width), f32),
            vmem((pad, 2 * width), f32),
            vmem((n, pad, 2 * width), f32),
            vmem((E_DEV * width, width), f32),
            vmem((E_DEV * width, 2 * width), f32),
            vmem((16, chunk), f32),
            vmem((n, 16, chunk), bf16),
            vmem((owned, out_lanes), f32),
            vmem((layers, owned // layers, out_lanes), f32),
            sems((E_DEV,)),
            sems((E_DEV,)),
            sems((3,)),
            sems((n,)),
            sems((n,)),
            sems((n,)),
            sems((n,)),
            sems((n // 2,)),
            sems((n // 2,)),
            sems((n // 2,)),
            sems((n // 2,)),
            sems((layers,)),
            sems((layers,)),
        ],
        compiler_params=pltpu.CompilerParams(
            collective_id=0, has_side_effects=True, vmem_limit_bytes=64 * 1024 * 1024 - 131072
        ),
        name="influence",
    )(
        x_act[0],
        g_out[0],
        jnp.swapaxes(proj_in, 1, 2)[0],
        jnp.swapaxes(proj_out, 1, 2)[0],
        queries[0],
        jnp.swapaxes(cand_ids, 1, 2)[0],
        cand_counts,
    )


def solution(mesh):
    return jax.shard_map(
        body,
        mesh=mesh,
        in_specs=(
            P("block", "dp", None),
            P("block", "dp", None),
            P("block", None, None),
            P("block", None, None),
            P("block", "dp", None),
            P("dp", None, None),
            P("dp", None),
        ),
        out_specs=P(("dp", "block"), None),
        check_vma=False,
    )
```
